32 devices in a mesh: fsdp: 8 (over y, x, core), tp: 4 (over z).
Axes of the slice: x: 2, y: 2, z: 4, core: 2. Of those that a mesh axis runs over, the one named last changes fastest.
Arguments:
- gradient: float32 [16384, 8192], P('fsdp', 'tp'), may hold values from -100 to 100
- sign_bits: int32 [8192, 128], P('tp'), may hold values 0 or 1
- block_column: int32 [64], P('tp'), may hold values from 0 to 3, as said below
Outputs:
- projected: float32 [512, 8192], P('fsdp', 'tp')
The draws below stay inside these ranges and needn't reach their ends.
Inputs may be any that keep to these rules, and one draw needn't show every extreme that they name: `block_column`: each of the 4 column blocks is chosen by at least two blocks of rows.
All inputs are finite; a program needn't handle non-finite values. No bound on the sum of `sign_bits` on one device may be relied on, other than what follows from the above.
Results may differ from the reference program's by a relative error of at most 0.000082.
Values sent between devices are 32-bit elements; how exact they have to be, the bound alone decides.
No kernel may reach another device: no remote copies, remote signals or barrier semaphores. Data moves between devices by JAX's collectives and lax.ppermute only.
A program may use at most 128 MiB of HBM per device.

```python
import math
import jax
import jax.numpy as jnp
from jax import lax

M = 16384
N = 8192
R = 512
BLK = 128


def draw_gradient(key, part):
    keys = jax.random.split(jax.random.fold_in(key, 7), 2)
    row_scale = jnp.exp(jax.random.uniform(keys[1], (M, 1), jnp.float32) * math.log(10.0))
    values = row_scale * jnp.clip(jax.random.normal(keys[0], (M, N), jnp.float32), -6.0, 6.0)
    return values.astype(jnp.float32)


def draw_block_column(key, part):
    block_count = N // BLK
    column_blocks = R // BLK
    keys = jax.random.split(jax.random.fold_in(key, 11), 2)
    base = jax.random.randint(keys[0], (block_count,), 0, column_blocks, dtype=jnp.int32)
    shuffled = jax.random.permutation(keys[1], block_count)
    forced = jnp.arange(2 * column_blocks, dtype=jnp.int32) % column_blocks
    base = base.at[shuffled[:2 * column_blocks]].set(forced)
    return base.astype(jnp.int32)


def set_ends(drawn, rng, low, top_value):
    longest = drawn.shape.index(max(drawn.shape))
    spots = []
    for shift in (0, 1):
        where = [jax.random.randint(jax.random.fold_in(rng, axis), (), 0, length) for axis, length in enumerate(drawn.shape)]
        where[longest] = (where[longest] + shift) % drawn.shape[longest]
        spots.append(tuple(where))
    return drawn.at[spots[0]].set(low).at[spots[1]].set(top_value)


def setup_inputs(seed: int = 0) -> dict:
    splits = jax.random.split(jax.random.key(seed), 4)
    gradient = draw_gradient(jax.random.fold_in(splits[3], 71), 0)
    sign_bits = set_ends((jax.random.randint(splits[1], (N, BLK), 0, 2) < 1).astype(jnp.int32), jax.random.fold_in(splits[1], 1), 0, 1)
    block_column = draw_block_column(jax.random.fold_in(splits[3], 71), 0)
    return {"gradient": gradient, "sign_bits": sign_bits, "block_column": block_column}


def reference(gradient, sign_bits, block_column):
    block_count = N // BLK
    column_blocks = R // BLK
    sign_table = (2 * sign_bits - 1).astype(jnp.float32).reshape(block_count, BLK, BLK)
    row_blocks = gradient.reshape(M, block_count, BLK)
    mixture = jnp.einsum('rbk,bkj->rbj', row_blocks, sign_table, precision=lax.Precision.HIGHEST)
    chosen = (block_column[:, None] == jnp.arange(column_blocks, dtype=jnp.int32)[None, :]).astype(jnp.float32)
    sketch = jnp.einsum('rbj,bc->rcj', mixture, chosen, precision=lax.Precision.HIGHEST).reshape(M, R)
    gram_sum = jnp.dot(sketch.T.astype(jnp.float32), sketch.astype(jnp.float32), precision=lax.Precision.HIGHEST, preferred_element_type=jnp.float32)
    lower_factor = jnp.linalg.cholesky(gram_sum)
    basis_rows = jax.scipy.linalg.solve_triangular(lower_factor, sketch.T, lower=True).T
    return jnp.dot(basis_rows.T.astype(jnp.float32), gradient.astype(jnp.float32), precision=lax.Precision.HIGHEST, preferred_element_type=jnp.float32)
```

```python
import functools

import jax
import jax.numpy as jnp
from jax import lax
from jax.experimental import pallas as pl
from jax.experimental.pallas import tpu as pltpu
from jax.sharding import PartitionSpec as P

R = 512
CHUNK = 64
GROUPS = (128, 128, 128, 128)
HIGHEST = lax.Precision.HIGHEST
NT = (((1,), (1,)), ((), ()))
VMEM_LIMIT = 48 * 1024 * 1024


def split(x):
    hi = x.astype(jnp.bfloat16)
    return hi, (x - hi.astype(jnp.float32)).astype(jnp.bfloat16)


def sketch_kernel(column_ref, bits_ref, g_ref, out_ref):
    b = pl.program_id(0)

    @pl.when(b == 0)
    def _():
        out_ref[...] = jnp.zeros_like(out_ref)

    width = bits_ref.shape[1]
    signs = (2 * bits_ref[...] - 1).astype(jnp.float32).T.astype(jnp.bfloat16)
    hi, lo = split(g_ref[...])
    product = lax.dot_general(
        jnp.concatenate([signs, signs], axis=1),
        jnp.concatenate([hi, lo], axis=1),
        NT,
        preferred_element_type=jnp.float32,
    )
    rows = pl.ds(pl.multiple_of(column_ref[b] * width, width), width)
    out_ref[rows, :] += product


def partial_sketch(gradient, sign_bits, block_column):
    row_count, col_count = gradient.shape
    width = sign_bits.shape[1]
    blocks = col_count // width
    return pl.pallas_call(
        sketch_kernel,
        grid_spec=pltpu.PrefetchScalarGridSpec(
            num_scalar_prefetch=1,
            grid=(blocks,),
            in_specs=[
                pl.BlockSpec((width, width), lambda b, c: (b, 0)),
                pl.BlockSpec((row_count, width), lambda b, c: (0, b)),
            ],
            out_specs=pl.BlockSpec((R, row_count), lambda b, c: (0, 0)),
        ),
        out_shape=jax.ShapeDtypeStruct((R, row_count), jnp.float32),
        compiler_params=pltpu.CompilerParams(vmem_limit_bytes=VMEM_LIMIT),
        cost_estimate=pl.CostEstimate(
            flops=4 * row_count * col_count * width, bytes_accessed=4 * row_count * col_count, transcendentals=0
        ),
    )(block_column, sign_bits, gradient)


def crossed_kernel(count, *refs):
    s_ref, earlier, g_ref, out_ref, gram_ref, s_scratch = (
        refs[0], refs[1 : 1 + count], refs[1 + count], refs[2 + count], refs[3 + count], refs[4 + count],
    )
    width = s_ref.shape[0]

    @pl.when(pl.program_id(0) == 0)
    def _():
        s_hi, s_lo = split(s_ref[...])
        s_scratch[:width, :] = s_hi
        s_scratch[width:, :] = s_lo
        at = 0
        for ref in (*earlier, s_ref):
            hi, lo = split(ref[...])
            both = lax.dot_general(s_scratch[...], hi, NT, preferred_element_type=jnp.float32)
            low = lax.dot_general(s_hi, lo, NT, preferred_element_type=jnp.float32)
            gram_ref[:, at : at + ref.shape[0]] = both[:width] + (both[width:] + low)
            at += ref.shape[0]

    hi, lo = split(g_ref[...])
    both = jnp.dot(s_scratch[...], hi, preferred_element_type=jnp.float32)
    low = jnp.dot(s_scratch[:width, :], lo, preferred_element_type=jnp.float32)
    out_ref[...] = both[:width] + (both[width:] + low)


def crossed_and_gram(s, earlier, gradient):
    width, row_count = s.shape
    col_count = gradient.shape[1]
    tile = min(256, col_count)
    gram_cols = width + sum(e.shape[0] for e in earlier)
    whole = lambda a: pl.BlockSpec(a.shape, lambda j: (0, 0))
    return pl.pallas_call(
        functools.partial(crossed_kernel, len(earlier)),
        grid=(col_count // tile,),
        in_specs=[whole(s), *(whole(e) for e in earlier), pl.BlockSpec((row_count, tile), lambda j: (0, j))],
        out_specs=[
            pl.BlockSpec((width, tile), lambda j: (0, j)),
            pl.BlockSpec((width, gram_cols), lambda j: (0, 0)),
        ],
        out_shape=[
            jax.ShapeDtypeStruct((width, col_count), jnp.float32),
            jax.ShapeDtypeStruct((width, gram_cols), jnp.float32),
        ],
        scratch_shapes=[pltpu.VMEM((2 * width, row_count), jnp.bfloat16)],
        compiler_params=pltpu.CompilerParams(vmem_limit_bytes=VMEM_LIMIT),
        cost_estimate=pl.CostEstimate(
            flops=6 * width * row_count * col_count, bytes_accessed=4 * row_count * col_count, transcendentals=0
        ),
    )(s, *earlier, gradient)


def mm(a, b, dims=(((1,), (0,)), ((), ()))):
    return lax.dot_general(a, b, dims, precision=HIGHEST, preferred_element_type=jnp.float32)


def inverse_factor(a):
    n = a.shape[0]
    row = lax.broadcasted_iota(jnp.int32, (n, n), 0)
    col = lax.broadcasted_iota(jnp.int32, (n, n), 1)
    right = jnp.where(row == col, 1.0, 0.0).astype(jnp.float32)
    pivots = jnp.ones((n, 1), jnp.float32)
    below = lax.broadcasted_iota(jnp.int32, (n, 1), 0)
    for j in range(n):
        pivot = a[j : j + 1, j : j + 1]
        column = a[:, j : j + 1]
        pivots = jnp.where(below == j, column, pivots)
        factor = jnp.where(below > j, column, 0.0) * (1.0 / pivot)
        right = right - factor * right[j : j + 1, :]
        a = a - factor * a[j : j + 1, :]
    return right * (1.0 / jnp.sqrt(pivots))


def finish_kernel(first, *refs):
    if first:
        gram_ref, c_ref, inv_ref, y_ref = refs
        inv = inverse_factor(gram_ref[...])
        inv_ref[...] = inv
        y_ref[...] = mm(inv, c_ref[...])
        return
    gram_ref, c_ref, before_ref, y_before_ref, inv_ref, y_ref = refs
    before = before_ref.shape[0]
    lower = mm(gram_ref[:, :before], before_ref[...], NT)
    inv = inverse_factor(gram_ref[:, before:] - mm(lower, lower, NT))
    inv_ref[:, :before] = -mm(inv, mm(lower, before_ref[...]))
    inv_ref[:, before:] = inv
    y_ref[...] = mm(inv, c_ref[...] - mm(lower, y_before_ref[...]))


def finish(gram, c, before, y_before):
    width, gram_cols = gram.shape
    first = before is None
    args = (gram, c) if first else (gram, c, before, y_before)
    vmem = pl.BlockSpec(memory_space=pltpu.VMEM)
    return pl.pallas_call(
        functools.partial(finish_kernel, first),
        in_specs=[vmem] * len(args),
        out_specs=[vmem, vmem],
        out_shape=[
            jax.ShapeDtypeStruct((width, gram_cols), jnp.float32),
            jax.ShapeDtypeStruct(c.shape, jnp.float32),
        ],
        compiler_params=pltpu.CompilerParams(vmem_limit_bytes=VMEM_LIMIT),
        cost_estimate=pl.CostEstimate(flops=10_000_000_000, bytes_accessed=1 << 20, transcendentals=0),
    )(*args)


class Order:
    def __init__(self):
        self.last = None

    def after(self, x):
        if self.last is None:
            return x
        tied, _ = lax.optimization_barrier((x, self.last))
        return tied

    def mark(self, x):
        self.last = x
        return x


def job(order, group, state, gradient, fsdp_size):
    s = order.after(group)
    crossed, gram = crossed_and_gram(s, state["sketch"], gradient)
    state["sketch"].append(s)
    order.mark(gram)
    me = lax.axis_index("fsdp")
    width = crossed.shape[0]
    hop = 1
    while hop < fsdp_size:
        bit = (me // hop) % 2
        half = crossed.shape[1] // 2
        away = lax.dynamic_slice(crossed, (0, (1 - bit) * half), (width, half))
        keep = lax.dynamic_slice(crossed, (0, bit * half), (width, half))
        pairs = [(i, i ^ hop) for i in range(fsdp_size)]
        got = lax.ppermute(jnp.concatenate([away, gram], axis=1), "fsdp", pairs)
        yield
        got = order.after(got)
        crossed = keep + got[:, :half]
        gram = gram + got[:, half:]
        order.mark(gram)
        hop *= 2
    before = state["inverse"]
    rows, y = finish(gram, crossed, before, state["y"])
    order.mark(y)
    if before is None:
        state["inverse"], state["y"] = rows, y
    else:
        size = before.shape[0]
        state["inverse"] = jnp.concatenate([jnp.pad(before, ((0, 0), (0, width))), rows], axis=0)
        state["y"] = jnp.concatenate([state["y"], y], axis=0)


def shards(tp_size, fsdp_size, gradient, sign_bits, block_column):
    partial = partial_sketch(gradient, sign_bits, block_column)
    count = R // CHUNK
    parts = [lax.slice_in_dim(partial, i * CHUNK, (i + 1) * CHUNK) for i in range(count)]
    order = Order()
    state = {"sketch": [], "inverse": None, "y": None}
    done, groups, jobs = [], list(GROUPS), []

    def arrived(chunk):
        done.append(chunk)
        if len(done) * CHUNK == groups[0]:
            jobs.append(job(order, jnp.concatenate(done, axis=0), state, gradient, fsdp_size))
            done.clear()
            groups.pop(0)

    def work():
        for j in list(jobs):
            if next(j, "end") == "end":
                jobs.remove(j)

    if tp_size == 4:
        t = lax.axis_index("tp")
        outer = (t == 0) | (t == tp_size - 1)
        ends, middle = [(0, 1), (1, 0), (2, 3), (3, 2)], [(1, 2), (2, 1)]
        folded, summed, from_end, from_middle = {}, {}, {}, {}
        for i in range(2):
            from_end[i] = lax.ppermute(parts[i], "tp", ends)
        order.mark(parts[1])
        for step in range(1, count + 4):
            i, j, q = step - 1, step - 2, step - 4
            if i < count:
                folded[i] = order.mark(parts[i] + order.after(from_end[i]))
                from_middle[i] = lax.ppermute(folded[i], "tp", middle)
            if q >= 0:
                arrived(jnp.where(outer, from_end[i], summed[q]))
            work()
            if 0 <= j < count:
                summed[j] = folded[j] + order.after(from_middle[j])
                send = jnp.where(outer, parts[step + 1], summed[j]) if step + 1 < count else summed[j]
                order.mark(send)
            elif step + 1 < count:
                send = parts[step + 1]
            else:
                continue
            if step + 1 > 1:
                from_end[step + 1] = lax.ppermute(send, "tp", ends)
    else:
        for part in parts:
            arrived(lax.psum(part, "tp"))
            work()
    while jobs:
        work()
    y = state["y"]
    moved = lax.all_to_all(y.reshape(fsdp_size, R // fsdp_size, y.shape[1]), "fsdp", 0, 0)
    bits = fsdp_size.bit_length() - 1
    flipped = [int(format(i, f"0{bits}b")[::-1], 2) if bits else 0 for i in range(fsdp_size)]
    return jnp.concatenate([moved[i] for i in flipped], axis=1)


def solution(mesh):
    return jax.shard_map(
        functools.partial(shards, mesh.shape["tp"], mesh.shape["fsdp"]),
        mesh=mesh,
        in_specs=(P("fsdp", "tp"), P("tp", None), P("tp")),
        out_specs=P("fsdp", "tp"),
        check_vma=False,
    )
```

```python
import functools

import jax
import jax.numpy as jnp
from jax import lax
from jax.experimental import pallas as pl
from jax.experimental.pallas import tpu as pltpu
from jax.sharding import PartitionSpec as P

R = 512
CHUNKS = (64,) * 8
GROUPS = (128,) * 4
PARTS_STEP = 3
HIGHEST = lax.Precision.HIGHEST
NT = (((1,), (1,)), ((), ()))
SKETCH_LIMIT = 36 * 1024 * 1024
SMALL_LIMIT = 12 * 1024 * 1024
PANEL = 8
SMALL_COST = pl.CostEstimate(flops=1, bytes_accessed=1, transcendentals=0)


def split(x):
    hi = x.astype(jnp.bfloat16)
    return hi, (x - hi.astype(jnp.float32)).astype(jnp.bfloat16)


def signs_of(bits):
    return (2 * bits - 1).astype(jnp.float32).T.astype(jnp.bfloat16)


def signed_sum(signs, hi, lo):
    return lax.dot_general(
        jnp.concatenate([signs, signs], axis=1),
        jnp.concatenate([hi, lo], axis=1),
        NT,
        preferred_element_type=jnp.float32,
    )


def first_sketch_kernel(column_ref, bits_ref, g_ref, out_ref, buffer, order, sem):
    width = bits_ref.shape[1]
    blocks = bits_ref.shape[0] // width
    depth = buffer.shape[0]

    def scan(b, found):
        here = column_ref[b] == 0

        @pl.when(here)
        def _():
            order[found] = b

        return found + jnp.where(here, 1, 0)

    count = lax.fori_loop(0, blocks, scan, 0)

    def fetch(i):
        slot = lax.rem(i, depth)
        start = pl.multiple_of(order[i] * width, width)
        return pltpu.make_async_copy(g_ref.at[:, pl.ds(start, width)], buffer.at[slot], sem.at[slot])

    for i in range(depth):
        @pl.when(i < count)
        def _():
            fetch(i).start()

    out_ref[...] = jnp.zeros_like(out_ref)

    def step(i, carry):
        fetch(i).wait()
        start = pl.multiple_of(order[i] * width, width)
        hi, lo = split(buffer[lax.rem(i, depth)])
        out_ref[...] += signed_sum(signs_of(bits_ref[pl.ds(start, width), :]), hi, lo)

        @pl.when(i + depth < count)
        def _():
            fetch(i + depth).start()

        return carry

    lax.fori_loop(0, count, step, 0)


def rest_sketch_kernel(column_ref, bits_ref, g_ref, out_ref, buffer, sem):
    width = bits_ref.shape[1]
    tile = buffer.shape[2]
    depth = buffer.shape[0]
    steps = g_ref.shape[1] // tile

    def fetch(i):
        return pltpu.make_async_copy(
            g_ref.at[:, i * tile : (i + 1) * tile], buffer.at[i % depth], sem.at[i % depth]
        )

    for i in range(min(depth, steps)):
        fetch(i).start()
    out_ref[...] = jnp.zeros_like(out_ref)
    for i in range(steps):
        fetch(i).wait()
        for q in range(tile // width):
            at = i * tile + q * width
            column = column_ref[at // width]

            @pl.when(column > 0)
            def _():
                hi, lo = split(buffer[i % depth, :, q * width : (q + 1) * width])
                signs = signs_of(bits_ref[at : at + width, :])
                rows = pl.ds(pl.multiple_of((column - 1) * width, width), width)
                out_ref[rows, :] += signed_sum(signs, hi, lo)

        if i + depth < steps:
            fetch(i + depth).start()


def parts_kernel(g_ref, hi_ref, lo_ref, buffer, sem):
    depth, _, tile = buffer.shape
    steps = g_ref.shape[1] // tile

    def fetch(i):
        return pltpu.make_async_copy(
            g_ref.at[:, i * tile : (i + 1) * tile], buffer.at[i % depth], sem.at[i % depth]
        )

    for i in range(min(depth, steps)):
        fetch(i).start()
    for i in range(steps):
        fetch(i).wait()
        cols = slice(i * tile, (i + 1) * tile)
        hi_ref[:, cols], lo_ref[:, cols] = split(buffer[i % depth])
        if i + depth < steps:
            fetch(i + depth).start()


VMEM = pl.BlockSpec(memory_space=pltpu.VMEM)
SKETCH_SPECS = [pl.BlockSpec(memory_space=pltpu.SMEM), VMEM, pl.BlockSpec(memory_space=pl.ANY)]


def partial_sketch(gradient, sign_bits, block_column):
    row_count, col_count = gradient.shape
    width = sign_bits.shape[1]
    blocks = col_count // width
    depth, tile = 4, 2 * width
    first = pl.pallas_call(
        first_sketch_kernel,
        in_specs=SKETCH_SPECS,
        out_specs=VMEM,
        out_shape=jax.ShapeDtypeStruct((width, row_count), jnp.float32),
        scratch_shapes=[
            pltpu.VMEM((depth, row_count, width), jnp.float32),
            pltpu.SMEM((blocks,), jnp.int32),
            pltpu.SemaphoreType.DMA((depth,)),
        ],
        compiler_params=pltpu.CompilerParams(vmem_limit_bytes=SKETCH_LIMIT),
        cost_estimate=SMALL_COST,
    )(block_column, sign_bits, gradient)
    rest = pl.pallas_call(
        rest_sketch_kernel,
        in_specs=SKETCH_SPECS,
        out_specs=VMEM,
        out_shape=jax.ShapeDtypeStruct((R - width, row_count), jnp.float32),
        scratch_shapes=[
            pltpu.VMEM((3, row_count, tile), jnp.float32),
            pltpu.SemaphoreType.DMA((3,)),
        ],
        compiler_params=pltpu.CompilerParams(vmem_limit_bytes=SKETCH_LIMIT),
        cost_estimate=SMALL_COST,
    )(block_column, sign_bits, gradient)
    return first, rest


def gradient_parts(gradient):
    row_count, col_count = gradient.shape
    half = jax.ShapeDtypeStruct((row_count, col_count), jnp.bfloat16)
    return pl.pallas_call(
        parts_kernel,
        in_specs=[pl.BlockSpec(memory_space=pl.ANY)],
        out_specs=[VMEM, VMEM],
        out_shape=[half, half],
        scratch_shapes=[
            pltpu.VMEM((3, row_count, min(256, col_count)), jnp.float32),
            pltpu.SemaphoreType.DMA((3,)),
        ],
        compiler_params=pltpu.CompilerParams(vmem_limit_bytes=SKETCH_LIMIT),
        cost_estimate=SMALL_COST,
    )(gradient)


def crossed_kernel(count, *refs):
    s_ref, earlier, (hi_ref, lo_ref, out_ref, gram_ref, both_ref) = refs[0], refs[1 : 1 + count], refs[1 + count :]
    width = s_ref.shape[0]
    col_count = hi_ref.shape[1]
    tile = min(512, col_count)
    s_hi, s_lo = split(s_ref[...])
    both_ref[:width, :] = s_hi
    both_ref[width:, :] = s_lo
    at = 0
    for ref in (*earlier, s_ref):
        hi, lo = split(ref[...])
        both = lax.dot_general(both_ref[...], hi, NT, preferred_element_type=jnp.float32)
        low = lax.dot_general(both_ref[:width, :], lo, NT, preferred_element_type=jnp.float32)
        gram_ref[:, at : at + ref.shape[0]] = both[:width] + (both[width:] + low)
        at += ref.shape[0]
    for start in range(0, col_count, tile):
        cols = slice(start, start + tile)
        both = jnp.dot(both_ref[...], hi_ref[:, cols], preferred_element_type=jnp.float32)
        low = jnp.dot(both_ref[:width, :], lo_ref[:, cols], preferred_element_type=jnp.float32)
        out_ref[:, cols] = both[:width] + (both[width:] + low)


def crossed_and_gram(s, earlier, hi, lo):
    width, row_count = s.shape
    col_count = hi.shape[1]
    gram_cols = width + sum(e.shape[0] for e in earlier)
    return pl.pallas_call(
        functools.partial(crossed_kernel, len(earlier)),
        in_specs=[VMEM] * (3 + len(earlier)),
        out_specs=[VMEM, VMEM],
        out_shape=[
            jax.ShapeDtypeStruct((width, col_count), jnp.float32),
            jax.ShapeDtypeStruct((width, gram_cols), jnp.float32),
        ],
        scratch_shapes=[pltpu.VMEM((2 * width, row_count), jnp.bfloat16)],
        compiler_params=pltpu.CompilerParams(vmem_limit_bytes=SMALL_LIMIT),
        cost_estimate=SMALL_COST,
    )(s, *earlier, hi, lo)


def mm(a, b, dims=(((1,), (0,)), ((), ()))):
    return lax.dot_general(a, b, dims, precision=HIGHEST, preferred_element_type=jnp.float32)


def inverse_factor(a):
    n = a.shape[0]
    row = lax.broadcasted_iota(jnp.int32, (n, n), 0)
    col = lax.broadcasted_iota(jnp.int32, (n, n), 1)
    x = jnp.where(row == col, 1.0, 0.0).astype(jnp.float32)
    out = []
    for j in range(0, n, PANEL):
        m = n - j
        cols = [jnp.broadcast_to(a[:, j + k : j + k + 1], (m, n)) for k in range(PANEL)]
        rows = [a[k : k + 1, :] for k in range(PANEL)]
        xrows = [x[k : k + 1, :] for k in range(PANEL)]
        d = [[cols[k][i : i + 1, :] for k in range(PANEL)] for i in range(PANEL)]
        inv = []
        for k in range(PANEL):
            inv.append(1.0 / d[k][k])
            for i in range(k + 1, PANEL):
                factor = d[i][k] * inv[k]
                rows[i] = rows[i] - factor * rows[k]
                xrows[i] = xrows[i] - factor * xrows[k]
                for q in range(i, PANEL):
                    d[q][i] = d[q][i] - factor * d[q][k]
                if m > PANEL:
                    cols[i] = cols[i] - factor * cols[k]
        out.append(jnp.concatenate([xrows[k] * jnp.sqrt(inv[k]) for k in range(PANEL)], axis=0))
        if m > PANEL:
            a, x = a[PANEL:], x[PANEL:]
            for k in range(PANEL):
                c = cols[k][PANEL:] * inv[k]
                a = a - c * rows[k]
                x = x - c * xrows[k]
    return jnp.concatenate(out, axis=0)


def finish_kernel(count, last, gram_ref, c_ref, *refs):
    inverses, ys, outs = refs[:count], refs[count : 2 * count], refs[2 * count :]
    before = gram_ref.shape[1] - gram_ref.shape[0]
    schur = gram_ref[:, before:]
    c = c_ref[...]
    lowers = []
    for inverse, y in zip(inverses, ys, strict=True):
        lower = mm(gram_ref[:, : inverse.shape[1]], inverse[...], NT)
        schur = schur - mm(lower, lower, NT)
        c = c - mm(lower, y[...])
        lowers.append(lower)
    inv = inverse_factor(schur)
    outs[0][...] = mm(inv, c)
    if last:
        return
    if count:
        outs[1][:, :before] = jnp.zeros((inv.shape[0], before), jnp.float32)
    for inverse, lower in zip(inverses, lowers, strict=True):
        outs[1][:, : inverse.shape[1]] -= mm(inv, mm(lower, inverse[...]))
    outs[1][:, before:] = inv


def finish(gram, c, inverses, ys, last):
    out_shape = [jax.ShapeDtypeStruct(c.shape, jnp.float32)]
    if not last:
        out_shape.append(jax.ShapeDtypeStruct(gram.shape, jnp.float32))
    args = (gram, c, *inverses, *ys)
    return pl.pallas_call(
        functools.partial(finish_kernel, len(inverses), last),
        in_specs=[VMEM] * len(args),
        out_specs=[VMEM] * len(out_shape),
        out_shape=out_shape,
        compiler_params=pltpu.CompilerParams(vmem_limit_bytes=SMALL_LIMIT),
        cost_estimate=SMALL_COST,
    )(*args)


class Order:
    def __init__(self):
        self.last = None

    def after(self, x):
        if self.last is None:
            return x
        tied, _ = lax.optimization_barrier((x, self.last))
        return tied

    def mark(self, x):
        self.last = x
        return x


def job(order, group, state, hi, lo, fsdp_size):
    s = group
    crossed, gram = crossed_and_gram(s, state["sketch"], hi, lo)
    state["sketch"].append(s)
    me = lax.axis_index("fsdp")
    width = crossed.shape[0]
    hop = 1
    while hop < fsdp_size:
        bit = (me // hop) % 2
        half = crossed.shape[1] // 2
        away = lax.dynamic_slice(crossed, (0, (1 - bit) * half), (width, half))
        keep = lax.dynamic_slice(crossed, (0, bit * half), (width, half))
        pairs = [(i, i ^ hop) for i in range(fsdp_size)]
        got = lax.ppermute(jnp.concatenate([away, gram], axis=1), "fsdp", pairs)
        crossed = keep + got[:, :half]
        gram = gram + got[:, half:]
        hop *= 2
    last = gram.shape[1] == R
    outs = finish(gram, crossed, state["inverse"], state["y"], last)
    state["y"].append(outs[0])
    yield
    state["inverse"].extend(outs[1:])


def shards(tp_size, fsdp_size, gradient, sign_bits, block_column):
    first, rest = partial_sketch(gradient, sign_bits, block_column)
    count = len(CHUNKS)
    parts, at = [], 0
    for size in CHUNKS:
        rows, start = (first, at) if at < first.shape[0] else (rest, at - first.shape[0])
        parts.append(lax.slice_in_dim(rows, start, start + size))
        at += size
    order = Order()
    state = {"sketch": [], "inverse": [], "y": []}
    done, groups, jobs = [], list(GROUPS), []

    def arrived(chunk):
        done.append(chunk)
        if sum(c.shape[0] for c in done) == groups[0]:
            group = jnp.concatenate(done, axis=0)
            jobs.append(job(order, group, state, *state["parts"], fsdp_size))
            done.clear()
            groups.pop(0)

    def work():
        for j in list(jobs):
            if next(j, "end") == "end":
                jobs.remove(j)

    if tp_size == 4:
        t = lax.axis_index("tp")
        outer = (t == 0) | (t == tp_size - 1)
        ends, middle = [(0, 1), (1, 0), (2, 3), (3, 2)], [(1, 2), (2, 1)]
        folded, summed, from_end, from_middle = {}, {}, {}, {}
        for i in range(2):
            from_end[i] = lax.ppermute(parts[i], "tp", ends)
        order.mark(parts[1])
        for step in range(1, count + 4):
            i, j, q = step - 1, step - 2, step - 4
            if i < count:
                folded[i] = order.mark(parts[i] + order.after(from_end[i])[: parts[i].shape[0]])
                from_middle[i] = lax.ppermute(folded[i], "tp", middle)
            if step == PARTS_STEP:
                state["parts"] = gradient_parts(order.after(gradient))
                order.mark(state["parts"][0])
            if q >= 0:
                shape = folded[q].shape[0]
                arrived(jnp.where(outer, from_end[i][:shape], summed[q]))
            work()
            send = parts[step + 1] if step + 1 < count else None
            if 0 <= j < count:
                summed[j] = folded[j] + order.after(from_middle[j])
                if send is None:
                    send = summed[j]
                else:
                    size = max(send.shape[0], summed[j].shape[0])
                    fit = lambda x: jnp.pad(x, ((0, size - x.shape[0]), (0, 0)))
                    send = jnp.where(outer, fit(send), fit(summed[j]))
                order.mark(send)
            if send is not None and step > 0 and step + 1 not in from_end:
                from_end[step + 1] = lax.ppermute(send, "tp", ends)
    else:
        state["parts"] = gradient_parts(gradient)
        for part in parts:
            arrived(lax.psum(part, "tp"))
            work()
    while jobs:
        work()
    y = jnp.concatenate(state["y"], axis=0)
    moved = lax.all_to_all(y.reshape(fsdp_size, R // fsdp_size, y.shape[1]), "fsdp", 0, 0)
    bits = fsdp_size.bit_length() - 1
    flipped = [int(format(i, f"0{bits}b")[::-1], 2) if bits else 0 for i in range(fsdp_size)]
    return jnp.concatenate([moved[i] for i in flipped], axis=1)


def solution(mesh):
    return jax.shard_map(
        functools.partial(shards, mesh.shape["tp"], mesh.shape["fsdp"]),
        mesh=mesh,
        in_specs=(P("fsdp", "tp"), P("tp", None), P("tp")),
        out_specs=P("fsdp", "tp"),
        check_vma=False,
    )
```

```python
import functools

import jax
import jax.numpy as jnp
from jax import lax
from jax.experimental import pallas as pl
from jax.experimental.pallas import tpu as pltpu
from jax.sharding import PartitionSpec as P

R = 512
CHUNKS = (64,) * 8
GROUPS = (128,) * 4
PARTS_STEP = 3
TIES = {10: (("crossed", 2), ("finished", 0)), 11: (("finished", 1),)}
HIGHEST = lax.Precision.HIGHEST
NT = (((1,), (1,)), ((), ()))
SKETCH_LIMIT = 36 * 1024 * 1024
PARTS_LIMIT = 28 * 1024 * 1024
SMALL_LIMIT = 12 * 1024 * 1024
PANEL = 8
SMALL_COST = pl.CostEstimate(flops=1, bytes_accessed=1, transcendentals=0)


def split(x):
    hi = x.astype(jnp.bfloat16)
    return hi, (x - hi.astype(jnp.float32)).astype(jnp.bfloat16)


def signs_of(bits):
    return (2 * bits - 1).astype(jnp.float32).T.astype(jnp.bfloat16)


def signed_sum(signs, hi, lo):
    return lax.dot_general(
        jnp.concatenate([signs, signs], axis=1),
        jnp.concatenate([hi, lo], axis=1),
        NT,
        preferred_element_type=jnp.float32,
    )


def first_sketch_kernel(column_ref, bits_ref, g_ref, out_ref, buffer, order, sem):
    width = bits_ref.shape[1]
    blocks = bits_ref.shape[0] // width
    depth = buffer.shape[0]

    def scan(b, found):
        here = column_ref[b] == 0

        @pl.when(here)
        def _():
            order[found] = b

        return found + jnp.where(here, 1, 0)

    count = lax.fori_loop(0, blocks, scan, 0)

    def fetch(i):
        slot = lax.rem(i, depth)
        start = pl.multiple_of(order[i] * width, width)
        return pltpu.make_async_copy(g_ref.at[:, pl.ds(start, width)], buffer.at[slot], sem.at[slot])

    for i in range(depth):
        @pl.when(i < count)
        def _():
            fetch(i).start()

    out_ref[...] = jnp.zeros_like(out_ref)

    def step(i, carry):
        fetch(i).wait()
        start = pl.multiple_of(order[i] * width, width)
        hi, lo = split(buffer[lax.rem(i, depth)])
        out_ref[...] += signed_sum(signs_of(bits_ref[pl.ds(start, width), :]), hi, lo)

        @pl.when(i + depth < count)
        def _():
            fetch(i + depth).start()

        return carry

    lax.fori_loop(0, count, step, 0)


def rest_sketch_kernel(column_ref, bits_ref, g_ref, out_ref, buffer, sem):
    width = bits_ref.shape[1]
    tile = buffer.shape[2]
    depth = buffer.shape[0]
    steps = g_ref.shape[1] // tile

    def fetch(i):
        return pltpu.make_async_copy(
            g_ref.at[:, i * tile : (i + 1) * tile], buffer.at[i % depth], sem.at[i % depth]
        )

    for i in range(min(depth, steps)):
        fetch(i).start()
    out_ref[...] = jnp.zeros_like(out_ref)
    for i in range(steps):
        fetch(i).wait()
        for q in range(tile // width):
            at = i * tile + q * width
            column = column_ref[at // width]

            @pl.when(column > 0)
            def _():
                hi, lo = split(buffer[i % depth, :, q * width : (q + 1) * width])
                signs = signs_of(bits_ref[at : at + width, :])
                rows = pl.ds(pl.multiple_of((column - 1) * width, width), width)
                out_ref[rows, :] += signed_sum(signs, hi, lo)

        if i + depth < steps:
            fetch(i + depth).start()


def parts_kernel(g_ref, hi_ref, lo_ref, buffer, sem):
    depth, _, tile = buffer.shape
    steps = g_ref.shape[1] // tile

    def fetch(i):
        return pltpu.make_async_copy(
            g_ref.at[:, i * tile : (i + 1) * tile], buffer.at[i % depth], sem.at[i % depth]
        )

    for i in range(min(depth, steps)):
        fetch(i).start()
    for i in range(steps):
        fetch(i).wait()
        cols = slice(i * tile, (i + 1) * tile)
        hi_ref[:, cols], lo_ref[:, cols] = split(buffer[i % depth])
        if i + depth < steps:
            fetch(i + depth).start()


VMEM = pl.BlockSpec(memory_space=pltpu.VMEM)
SKETCH_SPECS = [pl.BlockSpec(memory_space=pltpu.SMEM), VMEM, pl.BlockSpec(memory_space=pl.ANY)]


def partial_sketch(gradient, sign_bits, block_column):
    row_count, col_count = gradient.shape
    width = sign_bits.shape[1]
    blocks = col_count // width
    depth, tile = 4, 2 * width
    first = pl.pallas_call(
        first_sketch_kernel,
        in_specs=SKETCH_SPECS,
        out_specs=VMEM,
        out_shape=jax.ShapeDtypeStruct((width, row_count), jnp.float32),
        scratch_shapes=[
            pltpu.VMEM((depth, row_count, width), jnp.float32),
            pltpu.SMEM((blocks,), jnp.int32),
            pltpu.SemaphoreType.DMA((depth,)),
        ],
        compiler_params=pltpu.CompilerParams(vmem_limit_bytes=SKETCH_LIMIT),
        cost_estimate=SMALL_COST,
    )(block_column, sign_bits, gradient)
    rest = pl.pallas_call(
        rest_sketch_kernel,
        in_specs=SKETCH_SPECS,
        out_specs=VMEM,
        out_shape=jax.ShapeDtypeStruct((R - width, row_count), jnp.float32),
        scratch_shapes=[
            pltpu.VMEM((3, row_count, tile), jnp.float32),
            pltpu.SemaphoreType.DMA((3,)),
        ],
        compiler_params=pltpu.CompilerParams(vmem_limit_bytes=SKETCH_LIMIT),
        cost_estimate=SMALL_COST,
    )(block_column, sign_bits, gradient)
    return first, rest


def gradient_parts(gradient):
    row_count, col_count = gradient.shape
    half = jax.ShapeDtypeStruct((row_count, col_count), jnp.bfloat16)
    return pl.pallas_call(
        parts_kernel,
        in_specs=[pl.BlockSpec(memory_space=pl.ANY)],
        out_specs=[VMEM, VMEM],
        out_shape=[half, half],
        scratch_shapes=[
            pltpu.VMEM((3, row_count, min(256, col_count)), jnp.float32),
            pltpu.SemaphoreType.DMA((3,)),
        ],
        compiler_params=pltpu.CompilerParams(vmem_limit_bytes=PARTS_LIMIT),
        cost_estimate=SMALL_COST,
    )(gradient)


def crossed_kernel(count, *refs):
    s_ref, earlier, (hi_ref, lo_ref, out_ref, gram_ref, both_ref) = refs[0], refs[1 : 1 + count], refs[1 + count :]
    width = s_ref.shape[0]
    col_count = hi_ref.shape[1]
    tile = min(512, col_count)
    s_hi, s_lo = split(s_ref[...])
    both_ref[:width, :] = s_hi
    both_ref[width:, :] = s_lo
    at = 0
    for ref in (*earlier, s_ref):
        hi, lo = split(ref[...])
        both = lax.dot_general(both_ref[...], hi, NT, preferred_element_type=jnp.float32)
        low = lax.dot_general(both_ref[:width, :], lo, NT, preferred_element_type=jnp.float32)
        gram_ref[:, at : at + ref.shape[0]] = both[:width] + (both[width:] + low)
        at += ref.shape[0]
    for start in range(0, col_count, tile):
        cols = slice(start, start + tile)
        both = jnp.dot(both_ref[...], hi_ref[:, cols], preferred_element_type=jnp.float32)
        low = jnp.dot(both_ref[:width, :], lo_ref[:, cols], preferred_element_type=jnp.float32)
        out_ref[:, cols] = both[:width] + (both[width:] + low)


def crossed_and_gram(s, earlier, hi, lo):
    width, row_count = s.shape
    col_count = hi.shape[1]
    gram_cols = width + sum(e.shape[0] for e in earlier)
    return pl.pallas_call(
        functools.partial(crossed_kernel, len(earlier)),
        in_specs=[VMEM] * (3 + len(earlier)),
        out_specs=[VMEM, VMEM],
        out_shape=[
            jax.ShapeDtypeStruct((width, col_count), jnp.float32),
            jax.ShapeDtypeStruct((width, gram_cols), jnp.float32),
        ],
        scratch_shapes=[pltpu.VMEM((2 * width, row_count), jnp.bfloat16)],
        compiler_params=pltpu.CompilerParams(vmem_limit_bytes=SMALL_LIMIT),
        cost_estimate=SMALL_COST,
    )(s, *earlier, hi, lo)


def mm(a, b, dims=(((1,), (0,)), ((), ()))):
    return lax.dot_general(a, b, dims, precision=HIGHEST, preferred_element_type=jnp.float32)


def inverse_factor(a):
    n = a.shape[0]
    row = lax.broadcasted_iota(jnp.int32, (n, n), 0)
    col = lax.broadcasted_iota(jnp.int32, (n, n), 1)
    x = jnp.where(row == col, 1.0, 0.0).astype(jnp.float32)
    out = []
    for j in range(0, n, PANEL):
        m = n - j
        cols = [jnp.broadcast_to(a[:, j + k : j + k + 1], (m, n)) for k in range(PANEL)]
        rows = [a[k : k + 1, :] for k in range(PANEL)]
        xrows = [x[k : k + 1, :] for k in range(PANEL)]
        d = [[cols[k][i : i + 1, :] for k in range(PANEL)] for i in range(PANEL)]
        inv = []
        for k in range(PANEL):
            inv.append(1.0 / d[k][k])
            for i in range(k + 1, PANEL):
                factor = d[i][k] * inv[k]
                rows[i] = rows[i] - factor * rows[k]
                xrows[i] = xrows[i] - factor * xrows[k]
                for q in range(i, PANEL):
                    d[q][i] = d[q][i] - factor * d[q][k]
                if m > PANEL:
                    cols[i] = cols[i] - factor * cols[k]
        out.append(jnp.concatenate([xrows[k] * jnp.sqrt(inv[k]) for k in range(PANEL)], axis=0))
        if m > PANEL:
            a, x = a[PANEL:], x[PANEL:]
            for k in range(PANEL):
                c = cols[k][PANEL:] * inv[k]
                a = a - c * rows[k]
                x = x - c * xrows[k]
    return jnp.concatenate(out, axis=0)


def finish_kernel(count, last, gram_ref, c_ref, *refs):
    inverses, ys, outs = refs[:count], refs[count : 2 * count], refs[2 * count :]
    before = gram_ref.shape[1] - gram_ref.shape[0]
    schur = gram_ref[:, before:]
    c = c_ref[...]
    lowers = []
    for inverse, y in zip(inverses, ys, strict=True):
        lower = mm(gram_ref[:, : inverse.shape[1]], inverse[...], NT)
        schur = schur - mm(lower, lower, NT)
        c = c - mm(lower, y[...])
        lowers.append(lower)
    inv = inverse_factor(schur)
    outs[0][...] = mm(inv, c)
    if last:
        return
    if count:
        outs[1][:, :before] = jnp.zeros((inv.shape[0], before), jnp.float32)
    for inverse, lower in zip(inverses, lowers, strict=True):
        outs[1][:, : inverse.shape[1]] -= mm(inv, mm(lower, inverse[...]))
    outs[1][:, before:] = inv


def finish(gram, c, inverses, ys, last):
    out_shape = [jax.ShapeDtypeStruct(c.shape, jnp.float32)]
    if not last:
        out_shape.append(jax.ShapeDtypeStruct(gram.shape, jnp.float32))
    args = (gram, c, *inverses, *ys)
    return pl.pallas_call(
        functools.partial(finish_kernel, len(inverses), last),
        in_specs=[VMEM] * len(args),
        out_specs=[VMEM] * len(out_shape),
        out_shape=out_shape,
        compiler_params=pltpu.CompilerParams(vmem_limit_bytes=SMALL_LIMIT),
        cost_estimate=SMALL_COST,
    )(*args)


class Order:
    def __init__(self):
        self.last = None

    def after(self, x):
        if self.last is None:
            return x
        tied, _ = lax.optimization_barrier((x, self.last))
        return tied

    def also(self, x):
        self.last = (self.last, x)

    def mark(self, x):
        self.last = x
        return x


def job(order, group, state, hi, lo, fsdp_size):
    s = group
    crossed, gram = crossed_and_gram(s, state["sketch"], hi, lo)
    state["sketch"].append(s)
    state["crossed"].append(gram)
    me = lax.axis_index("fsdp")
    width = crossed.shape[0]
    hops = [1 << i for i in range(fsdp_size.bit_length() - 1)]
    if len(hops) == 3 and len(state["sketch"]) % 2 == 0:
        hops = [hops[0], hops[2], hops[1]]
        size = crossed.shape[1] // 8
        blocks = [crossed[:, i * size : (i + 1) * size] for i in (0, 2, 1, 3, 4, 6, 5, 7)]
        crossed = jnp.concatenate(blocks, axis=1)
    for hop in hops:
        bit = (me // hop) % 2
        half = crossed.shape[1] // 2
        away = lax.dynamic_slice(crossed, (0, (1 - bit) * half), (width, half))
        keep = lax.dynamic_slice(crossed, (0, bit * half), (width, half))
        pairs = [(i, i ^ hop) for i in range(fsdp_size)]
        got = lax.ppermute(jnp.concatenate([away, gram], axis=1), "fsdp", pairs)
        crossed = keep + got[:, :half]
        gram = gram + got[:, half:]
    last = gram.shape[1] == R
    outs = finish(gram, crossed, state["inverse"], state["y"], last)
    state["y"].append(outs[0])
    state["finished"].append(outs[0])
    yield
    state["inverse"].extend(outs[1:])


def shards(tp_size, fsdp_size, gradient, sign_bits, block_column):
    first, rest = partial_sketch(gradient, sign_bits, block_column)
    count = len(CHUNKS)
    parts, at = [], 0
    for size in CHUNKS:
        rows, start = (first, at) if at < first.shape[0] else (rest, at - first.shape[0])
        parts.append(lax.slice_in_dim(rows, start, start + size))
        at += size
    order = Order()
    state = {"sketch": [], "inverse": [], "y": [], "crossed": [], "finished": []}
    done, groups, jobs = [], list(GROUPS), []

    def arrived(chunk):
        done.append(chunk)
        if sum(c.shape[0] for c in done) == groups[0]:
            group = jnp.concatenate(done, axis=0)
            jobs.append(job(order, group, state, *state["parts"], fsdp_size))
            done.clear()
            groups.pop(0)

    def work():
        for j in list(jobs):
            if next(j, "end") == "end":
                jobs.remove(j)

    if tp_size == 4:
        t = lax.axis_index("tp")
        outer = (t == 0) | (t == tp_size - 1)
        ends, middle = [(0, 1), (1, 0), (2, 3), (3, 2)], [(1, 2), (2, 1)]
        folded, summed, from_end, from_middle = {}, {}, {}, {}
        for i in range(3):
            from_end[i] = lax.ppermute(parts[i], "tp", ends)
        order.mark(rest)
        for step in range(1, count + 4):
            i, j, q = step - 1, step - 2, step - 4
            for name, group in TIES.get(step, ()):
                order.also(state[name][group])
            if i < count:
                folded[i] = order.mark(parts[i] + order.after(from_end[i])[: parts[i].shape[0]])
                from_middle[i] = lax.ppermute(folded[i], "tp", middle)
            if q >= 0:
                shape = folded[q].shape[0]
                arrived(jnp.where(outer, order.after(from_end[i])[:shape], summed[q]))
            work()
            for j in ((0, 1) if step == 3 else (j,)):
                if step < 3 or j >= count:
                    continue
                summed[j] = folded[j] + order.after(from_middle[j])
                send = summed[j]
                if j + 3 < count:
                    size = max(parts[j + 3].shape[0], send.shape[0])
                    fit = lambda x: jnp.pad(x, ((0, size - x.shape[0]), (0, 0)))
                    send = jnp.where(outer, fit(parts[j + 3]), fit(send))
                order.mark(send)
                from_end[j + 3] = lax.ppermute(send, "tp", ends)
            if step == PARTS_STEP:
                state["parts"] = gradient_parts(order.after(gradient))
                order.mark(state["parts"][0])
    else:
        state["parts"] = gradient_parts(gradient)
        for part in parts:
            arrived(lax.psum(part, "tp"))
            work()
    while jobs:
        work()
    y = jnp.concatenate(state["y"], axis=0)
    moved = lax.all_to_all(y.reshape(fsdp_size, R // fsdp_size, y.shape[1]), "fsdp", 0, 0)
    bits = fsdp_size.bit_length() - 1
    flipped = [int(format(i, f"0{bits}b")[::-1], 2) if bits else 0 for i in range(fsdp_size)]
    return jnp.concatenate([moved[i] for i in flipped], axis=1)


def solution(mesh):
    return jax.shard_map(
        functools.partial(shards, mesh.shape["tp"], mesh.shape["fsdp"]),
        mesh=mesh,
        in_specs=(P("fsdp", "tp"), P("tp", None), P("tp")),
        out_specs=P("fsdp", "tp"),
        check_vma=False,
    )
```

```python
import functools

import jax
import jax.numpy as jnp
from jax import lax
from jax.experimental import pallas as pl
from jax.experimental.pallas import tpu as pltpu
from jax.sharding import PartitionSpec as P

R = 512
CHUNKS = (64,) * 8
GROUPS = (128,) * 4
PARTS_STEP = 3
TIES = {10: (("crossed", 2), ("finished", 0)), 11: (("finished", 1),)}
HIGHEST = lax.Precision.HIGHEST
NT = (((1,), (1,)), ((), ()))
SKETCH_LIMIT = 36 * 1024 * 1024
PARTS_LIMIT = 20 * 1024 * 1024
SMALL_LIMIT = 12 * 1024 * 1024
PANEL = 8
SMALL_COST = pl.CostEstimate(flops=1, bytes_accessed=1, transcendentals=0)


def split(x):
    hi = x.astype(jnp.bfloat16)
    return hi, (x - hi.astype(jnp.float32)).astype(jnp.bfloat16)


def signs_of(bits):
    return (2 * bits - 1).astype(jnp.float32).T.astype(jnp.bfloat16)


def signed_sum(signs, hi, lo):
    return lax.dot_general(
        jnp.concatenate([signs, signs], axis=1),
        jnp.concatenate([hi, lo], axis=1),
        NT,
        preferred_element_type=jnp.float32,
    )


def first_sketch_kernel(column_ref, bits_ref, g_ref, out_ref, buffer, order, sem):
    width = bits_ref.shape[1]
    blocks = bits_ref.shape[0] // width
    depth = buffer.shape[0]

    def scan(b, found):
        here = column_ref[b] == 0

        @pl.when(here)
        def _():
            order[found] = b

        return found + jnp.where(here, 1, 0)

    count = lax.fori_loop(0, blocks, scan, 0)

    def fetch(i):
        slot = lax.rem(i, depth)
        start = pl.multiple_of(order[i] * width, width)
        return pltpu.make_async_copy(g_ref.at[:, pl.ds(start, width)], buffer.at[slot], sem.at[slot])

    for i in range(depth):
        @pl.when(i < count)
        def _():
            fetch(i).start()

    out_ref[...] = jnp.zeros_like(out_ref)

    def step(i, carry):
        fetch(i).wait()
        start = pl.multiple_of(order[i] * width, width)
        hi, lo = split(buffer[lax.rem(i, depth)])
        out_ref[...] += signed_sum(signs_of(bits_ref[pl.ds(start, width), :]), hi, lo)

        @pl.when(i + depth < count)
        def _():
            fetch(i + depth).start()

        return carry

    lax.fori_loop(0, count, step, 0)


def rest_sketch_kernel(column_ref, bits_ref, g_ref, out_ref, buffer, sem):
    width = bits_ref.shape[1]
    tile = buffer.shape[2]
    depth = buffer.shape[0]
    steps = g_ref.shape[1] // tile

    def fetch(i):
        return pltpu.make_async_copy(
            g_ref.at[:, i * tile : (i + 1) * tile], buffer.at[i % depth], sem.at[i % depth]
        )

    for i in range(min(depth, steps)):
        fetch(i).start()
    out_ref[...] = jnp.zeros_like(out_ref)
    for i in range(steps):
        fetch(i).wait()
        for q in range(tile // width):
            at = i * tile + q * width
            column = column_ref[at // width]

            @pl.when(column > 0)
            def _():
                hi, lo = split(buffer[i % depth, :, q * width : (q + 1) * width])
                signs = signs_of(bits_ref[at : at + width, :])
                rows = pl.ds(pl.multiple_of((column - 1) * width, width), width)
                out_ref[rows, :] += signed_sum(signs, hi, lo)

        if i + depth < steps:
            fetch(i + depth).start()


def parts_kernel(g_ref, hi_ref, lo_ref, buffer, sem):
    depth, _, tile = buffer.shape
    steps = g_ref.shape[1] // tile

    def fetch(i):
        return pltpu.make_async_copy(
            g_ref.at[:, i * tile : (i + 1) * tile], buffer.at[i % depth], sem.at[i % depth]
        )

    for i in range(min(depth, steps)):
        fetch(i).start()
    for i in range(steps):
        fetch(i).wait()
        cols = slice(i * tile, (i + 1) * tile)
        hi_ref[:, cols], lo_ref[:, cols] = split(buffer[i % depth])
        if i + depth < steps:
            fetch(i + depth).start()


VMEM = pl.BlockSpec(memory_space=pltpu.VMEM)
SKETCH_SPECS = [pl.BlockSpec(memory_space=pltpu.SMEM), VMEM, pl.BlockSpec(memory_space=pl.ANY)]


def partial_sketch(gradient, sign_bits, block_column):
    row_count, col_count = gradient.shape
    width = sign_bits.shape[1]
    blocks = col_count // width
    depth, tile = 4, 2 * width
    first = pl.pallas_call(
        first_sketch_kernel,
        in_specs=SKETCH_SPECS,
        out_specs=VMEM,
        out_shape=jax.ShapeDtypeStruct((width, row_count), jnp.float32),
        scratch_shapes=[
            pltpu.VMEM((depth, row_count, width), jnp.float32),
            pltpu.SMEM((blocks,), jnp.int32),
            pltpu.SemaphoreType.DMA((depth,)),
        ],
        compiler_params=pltpu.CompilerParams(vmem_limit_bytes=SKETCH_LIMIT),
        cost_estimate=SMALL_COST,
    )(block_column, sign_bits, gradient)
    rest = pl.pallas_call(
        rest_sketch_kernel,
        in_specs=SKETCH_SPECS,
        out_specs=VMEM,
        out_shape=jax.ShapeDtypeStruct((R - width, row_count), jnp.float32),
        scratch_shapes=[
            pltpu.VMEM((3, row_count, tile), jnp.float32),
            pltpu.SemaphoreType.DMA((3,)),
        ],
        compiler_params=pltpu.CompilerParams(vmem_limit_bytes=SKETCH_LIMIT),
        cost_estimate=SMALL_COST,
    )(block_column, sign_bits, gradient)
    return first, rest


def gradient_parts(gradient):
    row_count, col_count = gradient.shape
    half = jax.ShapeDtypeStruct((row_count, col_count), jnp.bfloat16)
    return pl.pallas_call(
        parts_kernel,
        in_specs=[pl.BlockSpec(memory_space=pl.ANY)],
        out_specs=[VMEM, VMEM],
        out_shape=[half, half],
        scratch_shapes=[
            pltpu.VMEM((3, row_count, min(256, col_count)), jnp.float32),
            pltpu.SemaphoreType.DMA((3,)),
        ],
        compiler_params=pltpu.CompilerParams(vmem_limit_bytes=PARTS_LIMIT),
        cost_estimate=SMALL_COST,
    )(gradient)


def crossed_kernel(count, *refs):
    s_ref, earlier, (hi_ref, lo_ref, out_ref, gram_ref, both_ref) = refs[0], refs[1 : 1 + count], refs[1 + count :]
    width = s_ref.shape[0]
    col_count = hi_ref.shape[1]
    tile = min(512, col_count)
    s_hi, s_lo = split(s_ref[...])
    both_ref[:width, :] = s_hi
    both_ref[width:, :] = s_lo
    at = 0
    for ref in (*earlier, s_ref):
        hi, lo = split(ref[...])
        both = lax.dot_general(both_ref[...], hi, NT, preferred_element_type=jnp.float32)
        low = lax.dot_general(both_ref[:width, :], lo, NT, preferred_element_type=jnp.float32)
        gram_ref[:, at : at + ref.shape[0]] = both[:width] + (both[width:] + low)
        at += ref.shape[0]
    for start in range(0, col_count, tile):
        cols = slice(start, start + tile)
        both = jnp.dot(both_ref[...], hi_ref[:, cols], preferred_element_type=jnp.float32)
        low = jnp.dot(both_ref[:width, :], lo_ref[:, cols], preferred_element_type=jnp.float32)
        out_ref[:, cols] = both[:width] + (both[width:] + low)


def crossed_and_gram(s, earlier, hi, lo):
    width, row_count = s.shape
    col_count = hi.shape[1]
    gram_cols = width + sum(e.shape[0] for e in earlier)
    return pl.pallas_call(
        functools.partial(crossed_kernel, len(earlier)),
        in_specs=[VMEM] * (3 + len(earlier)),
        out_specs=[VMEM, VMEM],
        out_shape=[
            jax.ShapeDtypeStruct((width, col_count), jnp.float32),
            jax.ShapeDtypeStruct((width, gram_cols), jnp.float32),
        ],
        scratch_shapes=[pltpu.VMEM((2 * width, row_count), jnp.bfloat16)],
        compiler_params=pltpu.CompilerParams(vmem_limit_bytes=SMALL_LIMIT),
        cost_estimate=SMALL_COST,
    )(s, *earlier, hi, lo)


def mm(a, b, dims=(((1,), (0,)), ((), ()))):
    return lax.dot_general(a, b, dims, precision=HIGHEST, preferred_element_type=jnp.float32)


def inverse_factor(a):
    n = a.shape[0]
    row = lax.broadcasted_iota(jnp.int32, (n, n), 0)
    col = lax.broadcasted_iota(jnp.int32, (n, n), 1)
    x = jnp.where(row == col, 1.0, 0.0).astype(jnp.float32)
    out = []
    for j in range(0, n, PANEL):
        m = n - j
        cols = [jnp.broadcast_to(a[:, j + k : j + k + 1], (m, n)) for k in range(PANEL)]
        rows = [a[k : k + 1, :] for k in range(PANEL)]
        xrows = [x[k : k + 1, :] for k in range(PANEL)]
        d = [[cols[k][i : i + 1, :] for k in range(PANEL)] for i in range(PANEL)]
        inv = []
        for k in range(PANEL):
            inv.append(1.0 / d[k][k])
            for i in range(k + 1, PANEL):
                factor = d[i][k] * inv[k]
                rows[i] = rows[i] - factor * rows[k]
                xrows[i] = xrows[i] - factor * xrows[k]
                for q in range(i, PANEL):
                    d[q][i] = d[q][i] - factor * d[q][k]
                if m > PANEL:
                    cols[i] = cols[i] - factor * cols[k]
        out.append(jnp.concatenate([xrows[k] * jnp.sqrt(inv[k]) for k in range(PANEL)], axis=0))
        if m > PANEL:
            a, x = a[PANEL:], x[PANEL:]
            for k in range(PANEL):
                c = cols[k][PANEL:] * inv[k]
                a = a - c * rows[k]
                x = x - c * xrows[k]
    return jnp.concatenate(out, axis=0)


def finish_kernel(count, last, gram_ref, c_ref, *refs):
    inverses, ys, outs = refs[:count], refs[count : 2 * count], refs[2 * count :]
    before = gram_ref.shape[1] - gram_ref.shape[0]
    schur = gram_ref[:, before:]
    c = c_ref[...]
    lowers = []
    for inverse, y in zip(inverses, ys, strict=True):
        lower = mm(gram_ref[:, : inverse.shape[1]], inverse[...], NT)
        schur = schur - mm(lower, lower, NT)
        c = c - mm(lower, y[...])
        lowers.append(lower)
    inv = inverse_factor(schur)
    outs[0][...] = mm(inv, c)
    if last:
        return
    if count:
        outs[1][:, :before] = jnp.zeros((inv.shape[0], before), jnp.float32)
    for inverse, lower in zip(inverses, lowers, strict=True):
        outs[1][:, : inverse.shape[1]] -= mm(inv, mm(lower, inverse[...]))
    outs[1][:, before:] = inv


def finish(gram, c, inverses, ys, last):
    out_shape = [jax.ShapeDtypeStruct(c.shape, jnp.float32)]
    if not last:
        out_shape.append(jax.ShapeDtypeStruct(gram.shape, jnp.float32))
    args = (gram, c, *inverses, *ys)
    return pl.pallas_call(
        functools.partial(finish_kernel, len(inverses), last),
        in_specs=[VMEM] * len(args),
        out_specs=[VMEM] * len(out_shape),
        out_shape=out_shape,
        compiler_params=pltpu.CompilerParams(vmem_limit_bytes=SMALL_LIMIT),
        cost_estimate=SMALL_COST,
    )(*args)


class Order:
    def __init__(self):
        self.last = None

    def after(self, x):
        if self.last is None:
            return x
        tied, _ = lax.optimization_barrier((x, self.last))
        return tied

    def also(self, x):
        self.last = (self.last, x)

    def mark(self, x):
        self.last = x
        return x


def job(order, group, state, hi, lo, fsdp_size):
    s = group
    crossed, gram = crossed_and_gram(s, state["sketch"], hi, lo)
    state["sketch"].append(s)
    state["crossed"].append(gram)
    me = lax.axis_index("fsdp")
    width = crossed.shape[0]
    hops = [1 << i for i in range(fsdp_size.bit_length() - 1)]
    if len(hops) == 3 and len(state["sketch"]) in (1, len(GROUPS)):
        hops = [hops[0], hops[2], hops[1]]
        size = crossed.shape[1] // 8
        blocks = [crossed[:, i * size : (i + 1) * size] for i in (0, 2, 1, 3, 4, 6, 5, 7)]
        crossed = jnp.concatenate(blocks, axis=1)
    for hop in hops:
        bit = (me // hop) % 2
        half = crossed.shape[1] // 2
        away = lax.dynamic_slice(crossed, (0, (1 - bit) * half), (width, half))
        keep = lax.dynamic_slice(crossed, (0, bit * half), (width, half))
        pairs = [(i, i ^ hop) for i in range(fsdp_size)]
        got = lax.ppermute(jnp.concatenate([away, gram], axis=1), "fsdp", pairs)
        crossed = keep + got[:, :half]
        gram = gram + got[:, half:]
    last = gram.shape[1] == R
    outs = finish(gram, crossed, state["inverse"], state["y"], last)
    state["y"].append(outs[0])
    state["finished"].append(outs[0])
    yield
    state["inverse"].extend(outs[1:])


def shards(tp_size, fsdp_size, gradient, sign_bits, block_column):
    first, rest = partial_sketch(gradient, sign_bits, block_column)
    count = len(CHUNKS)
    parts, at = [], 0
    for size in CHUNKS:
        rows, start = (first, at) if at < first.shape[0] else (rest, at - first.shape[0])
        parts.append(lax.slice_in_dim(rows, start, start + size))
        at += size
    order = Order()
    state = {"sketch": [], "inverse": [], "y": [], "crossed": [], "finished": []}
    done, groups, jobs = [], list(GROUPS), []

    def arrived(chunk):
        done.append(chunk)
        if sum(c.shape[0] for c in done) == groups[0]:
            group = jnp.concatenate(done, axis=0)
            jobs.append(job(order, group, state, *state["parts"], fsdp_size))
            done.clear()
            groups.pop(0)

    def work():
        for j in list(jobs):
            if next(j, "end") == "end":
                jobs.remove(j)

    if tp_size == 4:
        t = lax.axis_index("tp")
        outer = (t == 0) | (t == tp_size - 1)
        ends, middle = [(0, 1), (1, 0), (2, 3), (3, 2)], [(1, 2), (2, 1)]
        folded, summed, from_end, from_middle = {}, {}, {}, {}
        for i in range(3):
            from_end[i] = lax.ppermute(parts[i], "tp", ends)
        order.mark(rest)
        for step in range(1, count + 4):
            i, j, q = step - 1, step - 2, step - 4
            for name, group in TIES.get(step, ()):
                order.also(state[name][group])
            if i < count:
                folded[i] = order.mark(parts[i] + order.after(from_end[i])[: parts[i].shape[0]])
                from_middle[i] = lax.ppermute(folded[i], "tp", middle)
            if q >= 0:
                shape = folded[q].shape[0]
                arrived(jnp.where(outer, order.after(from_end[i])[:shape], summed[q]))
            work()
            for j in ((0, 1) if step == 3 else (j,)):
                if step < 3 or j >= count:
                    continue
                summed[j] = folded[j] + order.after(from_middle[j])
                send = summed[j]
                if j + 3 < count:
                    size = max(parts[j + 3].shape[0], send.shape[0])
                    fit = lambda x: jnp.pad(x, ((0, size - x.shape[0]), (0, 0)))
                    send = jnp.where(outer, fit(parts[j + 3]), fit(send))
                order.mark(send)
                from_end[j + 3] = lax.ppermute(send, "tp", ends)
            if step == PARTS_STEP:
                state["parts"] = gradient_parts(order.after(gradient))
                order.mark(state["parts"][0])
    else:
        state["parts"] = gradient_parts(gradient)
        for part in parts:
            arrived(lax.psum(part, "tp"))
            work()
    while jobs:
        work()
    y = jnp.concatenate(state["y"], axis=0)
    moved = lax.all_to_all(y.reshape(fsdp_size, R // fsdp_size, y.shape[1]), "fsdp", 0, 0)
    bits = fsdp_size.bit_length() - 1
    flipped = [int(format(i, f"0{bits}b")[::-1], 2) if bits else 0 for i in range(fsdp_size)]
    return jnp.concatenate([moved[i] for i in flipped], axis=1)


def solution(mesh):
    return jax.shard_map(
        functools.partial(shards, mesh.shape["tp"], mesh.shape["fsdp"]),
        mesh=mesh,
        in_specs=(P("fsdp", "tp"), P("tp", None), P("tp")),
        out_specs=P("fsdp", "tp"),
        check_vma=False,
    )
```

```python
import functools

import jax
import jax.numpy as jnp
from jax import lax
from jax.experimental import pallas as pl
from jax.experimental.pallas import tpu as pltpu
from jax.sharding import PartitionSpec as P

R = 512
CHUNKS = (64,) * 8
GROUPS = (128,) * 4
PARTS_STEP = 3
TIES = {10: (("crossed", 2), ("finished", 0)), 11: (("finished", 1),)}
HIGHEST = lax.Precision.HIGHEST
NT = (((1,), (1,)), ((), ()))
SKETCH_LIMIT = 36 * 1024 * 1024
PARTS_LIMIT = 20 * 1024 * 1024
SMALL_LIMIT = 12 * 1024 * 1024
PANEL = 8
SMALL_COST = pl.CostEstimate(flops=1, bytes_accessed=1, transcendentals=0)


def split(x):
    hi = x.astype(jnp.bfloat16)
    return hi, (x - hi.astype(jnp.float32)).astype(jnp.bfloat16)


def signs_of(bits):
    return (2 * bits - 1).astype(jnp.float32).T.astype(jnp.bfloat16)


def signed_sum(signs, hi, lo):
    return lax.dot_general(
        jnp.concatenate([signs, signs], axis=1),
        jnp.concatenate([hi, lo], axis=1),
        NT,
        preferred_element_type=jnp.float32,
    )


def first_sketch_kernel(column_ref, bits_ref, g_ref, out_ref, buffer, order, sem):
    width = bits_ref.shape[1]
    blocks = bits_ref.shape[0] // width
    depth = buffer.shape[0]

    def scan(b, found):
        here = column_ref[b] == 0

        @pl.when(here)
        def _():
            order[found] = b

        return found + jnp.where(here, 1, 0)

    count = lax.fori_loop(0, blocks, scan, 0)

    def fetch(i):
        slot = lax.rem(i, depth)
        start = pl.multiple_of(order[i] * width, width)
        return pltpu.make_async_copy(g_ref.at[:, pl.ds(start, width)], buffer.at[slot], sem.at[slot])

    for i in range(depth):
        @pl.when(i < count)
        def _():
            fetch(i).start()

    out_ref[...] = jnp.zeros_like(out_ref)

    def step(i, carry):
        fetch(i).wait()
        start = pl.multiple_of(order[i] * width, width)
        hi, lo = split(buffer[lax.rem(i, depth)])
        out_ref[...] += signed_sum(signs_of(bits_ref[pl.ds(start, width), :]), hi, lo)

        @pl.when(i + depth < count)
        def _():
            fetch(i + depth).start()

        return carry

    lax.fori_loop(0, count, step, 0)


def rest_sketch_kernel(column_ref, bits_ref, g_ref, out_ref, buffer, sem):
    width = bits_ref.shape[1]
    tile = buffer.shape[2]
    depth = buffer.shape[0]
    steps = g_ref.shape[1] // tile

    def fetch(i):
        return pltpu.make_async_copy(
            g_ref.at[:, i * tile : (i + 1) * tile], buffer.at[i % depth], sem.at[i % depth]
        )

    for i in range(min(depth, steps)):
        fetch(i).start()
    out_ref[...] = jnp.zeros_like(out_ref)
    for i in range(steps):
        fetch(i).wait()
        for q in range(tile // width):
            at = i * tile + q * width
            column = column_ref[at // width]

            @pl.when(column > 0)
            def _():
                hi, lo = split(buffer[i % depth, :, q * width : (q + 1) * width])
                signs = signs_of(bits_ref[at : at + width, :])
                rows = pl.ds(pl.multiple_of((column - 1) * width, width), width)
                out_ref[rows, :] += signed_sum(signs, hi, lo)

        if i + depth < steps:
            fetch(i + depth).start()


def parts_kernel(g_ref, hi_ref, lo_ref, buffer, sem):
    depth, _, tile = buffer.shape
    steps = g_ref.shape[1] // tile

    def fetch(i):
        return pltpu.make_async_copy(
            g_ref.at[:, i * tile : (i + 1) * tile], buffer.at[i % depth], sem.at[i % depth]
        )

    for i in range(min(depth, steps)):
        fetch(i).start()
    for i in range(steps):
        fetch(i).wait()
        cols = slice(i * tile, (i + 1) * tile)
        hi_ref[:, cols], lo_ref[:, cols] = split(buffer[i % depth])
        if i + depth < steps:
            fetch(i + depth).start()


VMEM = pl.BlockSpec(memory_space=pltpu.VMEM)
SKETCH_SPECS = [pl.BlockSpec(memory_space=pltpu.SMEM), VMEM, pl.BlockSpec(memory_space=pl.ANY)]


def partial_sketch(gradient, sign_bits, block_column):
    row_count, col_count = gradient.shape
    width = sign_bits.shape[1]
    blocks = col_count // width
    depth, tile = 4, 2 * width
    first = pl.pallas_call(
        first_sketch_kernel,
        in_specs=SKETCH_SPECS,
        out_specs=VMEM,
        out_shape=jax.ShapeDtypeStruct((width, row_count), jnp.float32),
        scratch_shapes=[
            pltpu.VMEM((depth, row_count, width), jnp.float32),
            pltpu.SMEM((blocks,), jnp.int32),
            pltpu.SemaphoreType.DMA((depth,)),
        ],
        compiler_params=pltpu.CompilerParams(vmem_limit_bytes=SKETCH_LIMIT),
        cost_estimate=SMALL_COST,
    )(block_column, sign_bits, gradient)
    rest = pl.pallas_call(
        rest_sketch_kernel,
        in_specs=SKETCH_SPECS,
        out_specs=VMEM,
        out_shape=jax.ShapeDtypeStruct((R - width, row_count), jnp.float32),
        scratch_shapes=[
            pltpu.VMEM((3, row_count, tile), jnp.float32),
            pltpu.SemaphoreType.DMA((3,)),
        ],
        compiler_params=pltpu.CompilerParams(vmem_limit_bytes=SKETCH_LIMIT),
        cost_estimate=SMALL_COST,
    )(block_column, sign_bits, gradient)
    return first, rest


def gradient_parts(gradient):
    row_count, col_count = gradient.shape
    half = jax.ShapeDtypeStruct((row_count, col_count), jnp.bfloat16)
    return pl.pallas_call(
        parts_kernel,
        in_specs=[pl.BlockSpec(memory_space=pl.ANY)],
        out_specs=[VMEM, VMEM],
        out_shape=[half, half],
        scratch_shapes=[
            pltpu.VMEM((3, row_count, min(256, col_count)), jnp.float32),
            pltpu.SemaphoreType.DMA((3,)),
        ],
        compiler_params=pltpu.CompilerParams(vmem_limit_bytes=PARTS_LIMIT),
        cost_estimate=SMALL_COST,
    )(gradient)


def crossed_kernel(count, *refs):
    s_ref, earlier, (hi_ref, lo_ref, out_ref, gram_ref, both_ref) = refs[0], refs[1 : 1 + count], refs[1 + count :]
    width = s_ref.shape[0]
    col_count = hi_ref.shape[1]
    tile = min(512, col_count)
    s_hi, s_lo = split(s_ref[...])
    both_ref[:width, :] = s_hi
    both_ref[width:, :] = s_lo
    at = 0
    for ref in (*earlier, s_ref):
        hi, lo = split(ref[...])
        both = lax.dot_general(both_ref[...], hi, NT, preferred_element_type=jnp.float32)
        low = lax.dot_general(both_ref[:width, :], lo, NT, preferred_element_type=jnp.float32)
        gram_ref[:, at : at + ref.shape[0]] = both[:width] + (both[width:] + low)
        at += ref.shape[0]
    for start in range(0, col_count, tile):
        cols = slice(start, start + tile)
        both = jnp.dot(both_ref[...], hi_ref[:, cols], preferred_element_type=jnp.float32)
        low = jnp.dot(both_ref[:width, :], lo_ref[:, cols], preferred_element_type=jnp.float32)
        out_ref[:, cols] = both[:width] + (both[width:] + low)


def crossed_and_gram(s, earlier, hi, lo):
    width, row_count = s.shape
    col_count = hi.shape[1]
    gram_cols = width + sum(e.shape[0] for e in earlier)
    return pl.pallas_call(
        functools.partial(crossed_kernel, len(earlier)),
        in_specs=[VMEM] * (3 + len(earlier)),
        out_specs=[VMEM, VMEM],
        out_shape=[
            jax.ShapeDtypeStruct((width, col_count), jnp.float32),
            jax.ShapeDtypeStruct((width, gram_cols), jnp.float32),
        ],
        scratch_shapes=[pltpu.VMEM((2 * width, row_count), jnp.bfloat16)],
        compiler_params=pltpu.CompilerParams(vmem_limit_bytes=SMALL_LIMIT),
        cost_estimate=SMALL_COST,
    )(s, *earlier, hi, lo)


def mm(a, b, dims=(((1,), (0,)), ((), ()))):
    return lax.dot_general(a, b, dims, precision=HIGHEST, preferred_element_type=jnp.float32)


def mm3(a, b):
    (a_hi, a_lo), (b_hi, b_lo) = split(a), split(b)
    dot = functools.partial(jnp.dot, preferred_element_type=jnp.float32)
    return dot(a_hi, b_hi) + (dot(a_hi, b_lo) + dot(a_lo, b_hi))


def inverse_factor(a):
    n = a.shape[0]
    row = lax.broadcasted_iota(jnp.int32, (n, n), 0)
    col = lax.broadcasted_iota(jnp.int32, (n, n), 1)
    x = jnp.where(row == col, 1.0, 0.0).astype(jnp.float32)
    out = []
    for j in range(0, n, PANEL):
        m = n - j
        cols = [jnp.broadcast_to(a[:, j + k : j + k + 1], (m, n)) for k in range(PANEL)]
        rows = [a[k : k + 1, :] for k in range(PANEL)]
        xrows = [x[k : k + 1, :] for k in range(PANEL)]
        d = [[cols[k][i : i + 1, :] for k in range(PANEL)] for i in range(PANEL)]
        inv = []
        for k in range(PANEL):
            inv.append(1.0 / d[k][k])
            for i in range(k + 1, PANEL):
                factor = d[i][k] * inv[k]
                rows[i] = rows[i] - factor * rows[k]
                xrows[i] = xrows[i] - factor * xrows[k]
                for q in range(i, PANEL):
                    d[q][i] = d[q][i] - factor * d[q][k]
                if m > PANEL:
                    cols[i] = cols[i] - factor * cols[k]
        out.append(jnp.concatenate([xrows[k] * jnp.sqrt(inv[k]) for k in range(PANEL)], axis=0))
        if m > PANEL:
            a, x = a[PANEL:], x[PANEL:]
            for k in range(PANEL):
                c = cols[k][PANEL:] * inv[k]
                a = a - c * rows[k]
                x = x - c * xrows[k]
    return jnp.concatenate(out, axis=0)


def finish_kernel(count, last, gram_ref, c_ref, *refs):
    inverses, ys, outs = refs[:count], refs[count : 2 * count], refs[2 * count :]
    before = gram_ref.shape[1] - gram_ref.shape[0]
    schur = gram_ref[:, before:]
    c = c_ref[...]
    lowers = []
    for inverse, y in zip(inverses, ys, strict=True):
        lower = mm(gram_ref[:, : inverse.shape[1]], inverse[...], NT)
        schur = schur - mm(lower, lower, NT)
        c = c - mm3(lower, y[...])
        lowers.append(lower)
    inv = inverse_factor(schur)
    outs[0][...] = mm3(inv, c)
    if last:
        return
    if count:
        outs[1][:, :before] = jnp.zeros((inv.shape[0], before), jnp.float32)
    for inverse, lower in zip(inverses, lowers, strict=True):
        outs[1][:, : inverse.shape[1]] -= mm(inv, mm(lower, inverse[...]))
    outs[1][:, before:] = inv


def finish(gram, c, inverses, ys, last):
    out_shape = [jax.ShapeDtypeStruct(c.shape, jnp.float32)]
    if not last:
        out_shape.append(jax.ShapeDtypeStruct(gram.shape, jnp.float32))
    args = (gram, c, *inverses, *ys)
    return pl.pallas_call(
        functools.partial(finish_kernel, len(inverses), last),
        in_specs=[VMEM] * len(args),
        out_specs=[VMEM] * len(out_shape),
        out_shape=out_shape,
        compiler_params=pltpu.CompilerParams(vmem_limit_bytes=SMALL_LIMIT),
        cost_estimate=SMALL_COST,
    )(*args)


class Order:
    def __init__(self):
        self.last = None

    def after(self, x):
        if self.last is None:
            return x
        tied, _ = lax.optimization_barrier((x, self.last))
        return tied

    def also(self, x):
        self.last = (self.last, x)

    def mark(self, x):
        self.last = x
        return x


def job(order, group, state, hi, lo, fsdp_size):
    s = group
    crossed, gram = crossed_and_gram(s, state["sketch"], hi, lo)
    state["sketch"].append(s)
    state["crossed"].append(gram)
    me = lax.axis_index("fsdp")
    width = crossed.shape[0]
    hops = [1 << i for i in range(fsdp_size.bit_length() - 1)]
    if len(hops) == 3 and len(state["sketch"]) in (1, len(GROUPS)):
        hops = [hops[0], hops[2], hops[1]]
        size = crossed.shape[1] // 8
        blocks = [crossed[:, i * size : (i + 1) * size] for i in (0, 2, 1, 3, 4, 6, 5, 7)]
        crossed = jnp.concatenate(blocks, axis=1)
    for hop in hops:
        bit = (me // hop) % 2
        half = crossed.shape[1] // 2
        away = lax.dynamic_slice(crossed, (0, (1 - bit) * half), (width, half))
        keep = lax.dynamic_slice(crossed, (0, bit * half), (width, half))
        pairs = [(i, i ^ hop) for i in range(fsdp_size)]
        got = lax.ppermute(jnp.concatenate([away, gram], axis=1), "fsdp", pairs)
        crossed = keep + got[:, :half]
        gram = gram + got[:, half:]
    last = gram.shape[1] == R
    outs = finish(gram, crossed, state["inverse"], state["y"], last)
    state["y"].append(outs[0])
    state["finished"].append(outs[0])
    yield
    state["inverse"].extend(outs[1:])


def shards(tp_size, fsdp_size, gradient, sign_bits, block_column):
    first, rest = partial_sketch(gradient, sign_bits, block_column)
    count = len(CHUNKS)
    parts, at = [], 0
    for size in CHUNKS:
        rows, start = (first, at) if at < first.shape[0] else (rest, at - first.shape[0])
        parts.append(lax.slice_in_dim(rows, start, start + size))
        at += size
    order = Order()
    state = {"sketch": [], "inverse": [], "y": [], "crossed": [], "finished": []}
    done, groups, jobs = [], list(GROUPS), []

    def arrived(chunk):
        done.append(chunk)
        if sum(c.shape[0] for c in done) == groups[0]:
            group = jnp.concatenate(done, axis=0)
            jobs.append(job(order, group, state, *state["parts"], fsdp_size))
            done.clear()
            groups.pop(0)

    def work():
        for j in list(jobs):
            if next(j, "end") == "end":
                jobs.remove(j)

    if tp_size == 4:
        t = lax.axis_index("tp")
        outer = (t == 0) | (t == tp_size - 1)
        ends, middle = [(0, 1), (1, 0), (2, 3), (3, 2)], [(1, 2), (2, 1)]
        folded, summed, from_end, from_middle = {}, {}, {}, {}
        for i in range(3):
            from_end[i] = lax.ppermute(parts[i], "tp", ends)
        order.mark(rest)
        for step in range(1, count + 4):
            i, j, q = step - 1, step - 2, step - 4
            for name, group in TIES.get(step, ()):
                order.also(state[name][group])
            if i < count:
                folded[i] = order.mark(parts[i] + order.after(from_end[i])[: parts[i].shape[0]])
                from_middle[i] = lax.ppermute(folded[i], "tp", middle)
            if q >= 0:
                shape = folded[q].shape[0]
                arrived(jnp.where(outer, order.after(from_end[i])[:shape], summed[q]))
            work()
            for j in ((0, 1) if step == 3 else (j,)):
                if step < 3 or j >= count:
                    continue
                summed[j] = folded[j] + order.after(from_middle[j])
                send = summed[j]
                if j + 3 < count:
                    size = max(parts[j + 3].shape[0], send.shape[0])
                    fit = lambda x: jnp.pad(x, ((0, size - x.shape[0]), (0, 0)))
                    send = jnp.where(outer, fit(parts[j + 3]), fit(send))
                order.mark(send)
                from_end[j + 3] = lax.ppermute(send, "tp", ends)
            if step == PARTS_STEP:
                state["parts"] = gradient_parts(order.after(gradient))
                order.mark(state["parts"][0])
    else:
        state["parts"] = gradient_parts(gradient)
        for part in parts:
            arrived(lax.psum(part, "tp"))
            work()
    while jobs:
        work()
    y = jnp.concatenate(state["y"], axis=0)
    moved = lax.all_to_all(y.reshape(fsdp_size, R // fsdp_size, y.shape[1]), "fsdp", 0, 0)
    bits = fsdp_size.bit_length() - 1
    flipped = [int(format(i, f"0{bits}b")[::-1], 2) if bits else 0 for i in range(fsdp_size)]
    return jnp.concatenate([moved[i] for i in flipped], axis=1)


def solution(mesh):
    return jax.shard_map(
        functools.partial(shards, mesh.shape["tp"], mesh.shape["fsdp"]),
        mesh=mesh,
        in_specs=(P("fsdp", "tp"), P("tp", None), P("tp")),
        out_specs=P("fsdp", "tp"),
        check_vma=False,
    )
```
